128 devices in a mesh: row: 8 (over x_lo, y), col: 8 (over x_hi, z), depth: 2 (over core).
Axes of the slice: x: 4 (x_hi: 2, x_lo: 2; x = x_hi * 2 + x_lo), y: 4, z: 4, core: 2. Of those that a mesh axis runs over, the one named last changes fastest.
Arguments:
- half_slabs: bfloat16 [4, 12000, 1536], P('depth', 'row', 'col'), may hold values from -0.67578125 to 0.67578125
Outputs:
- exchange_matrix: float32 [12000, 12000], P('row', ('col', 'depth'))
The draws below stay inside these ranges and needn't reach their ends.
All inputs are finite; a program needn't handle non-finite values.
Results may differ from the reference program's by a relative error of at most 0.0003.
Values may be sent and summed in bfloat16 or wider, within the bound.
No kernel may reach another device: no remote copies, remote signals or barrier semaphores. Data moves between devices by JAX's collectives and lax.ppermute only.
A program may use at most 128 MiB of HBM per device.

```python
import jax
import jax.numpy as jnp
from jax import lax

NBF = 12000
NOCC = 1536
Q_WIN = 4


def steps_of(key, dims, shards, low, high):
    def one(axis_at, parts):
        heights = jax.random.uniform(jax.random.fold_in(jax.random.fold_in(key, 6), axis_at), (parts,), jnp.float32, low / len(shards), high / len(shards))
        return jnp.repeat(jnp.exp(heights), dims[axis_at] // parts).reshape((-1,) + (1,) * (len(dims) - axis_at - 1))

    level = one(*shards[0])
    for cut in shards[1:]:
        level = level * one(*cut)
    return level


def scatter_about(own_key, dims, deviation, most, shards=(), dtype=jnp.bfloat16):
    gain = steps_of(own_key, dims, shards, -0.22, 0.18) if shards else 1.0
    entries = jax.random.normal(own_key, dims, jnp.float32) * deviation * gain
    return jnp.minimum(jnp.maximum(entries, -most), most).astype(dtype)


def setup_inputs(seed: int = 0) -> dict:
    keys = jax.random.split(jax.random.key(seed), 2)
    return {
        "half_slabs": scatter_about(keys[0], (Q_WIN, NBF, NOCC), ((Q_WIN * NOCC) ** -0.25), 0.67578125, ((0, 2), (1, 8), (2, 8))),
    }


def reference(half_slabs):
    def accumulate(carry, slab_rows):
        return carry + jnp.dot(slab_rows, slab_rows.T, preferred_element_type=jnp.float32), None

    start_total = jnp.zeros((NBF, NBF), jnp.float32)
    exchange_total, unused_out = lax.scan(accumulate, start_total, half_slabs)
    return exchange_total
```

```python
import itertools

import jax
import jax.numpy as jnp
import numpy as np
from jax import lax
from jax.experimental import pallas as pl
from jax.experimental.pallas import tpu as pltpu
from jax.sharding import Mesh
from jax.sharding import PartitionSpec as P

AXES = ("xl", "y", "xh", "z", "d")
SIZES = (2, 4, 2, 4, 2)
GAMMA = (0, 2)
ROWS, COLS, PART = 1536, 768, 384
TILE = 256


def perm(target):
    out = []
    for at in itertools.product(*map(range, SIZES)):
        to = target(*at)
        out.append((int(np.ravel_multi_index(at, SIZES)), int(np.ravel_multi_index(to, SIZES))))
    return out


def turn(cross):
    def target(xl, y, xh, z, d):
        e = 1 - d if cross else d
        return xh ^ e, (GAMMA[e] - y - z) % 4, xl, y, e

    return perm(target)


Z_RING = perm(lambda xl, y, xh, z, d: (xl, y, xh, (z + 1 - 2 * d) % 4, d))
Y_RING = perm(lambda xl, y, xh, z, d: (xl, (y + 1 - 2 * d) % 4, xh, z, d))
X_FAR = perm(lambda xl, y, xh, z, d: (xl, y, 1 - xh, z, d))
X_NEAR = perm(lambda xl, y, xh, z, d: (1 - xl, y, xh, z, d))
CORES = perm(lambda xl, y, xh, z, d: (xl, y, xh, z, 1 - d))


def send(block, pairs):
    return lax.ppermute(block, AXES, pairs)


def multiply_kernel(which, *refs):
    own, other, columns = refs[:8], refs[8:16], refs[16:24]
    out, lhs, rhs, lhs_sem, rhs_sem = refs[24:]
    tile = pl.program_id(0)
    tiles = pl.num_programs(0)

    def lhs_copy(part, source, at):
        rows = pl.ds(at * TILE, TILE)
        return pltpu.make_async_copy(
            source.at[rows], lhs.at[rows, pl.ds(part * PART, PART)], lhs_sem.at[part, at]
        )

    def rhs_copy(piece):
        return pltpu.make_async_copy(
            columns[piece], rhs.at[pl.ds(piece * 2 * PART, 2 * PART)], rhs_sem.at[piece]
        )

    @pl.when(tile == 0)
    def _():
        for piece in range(8):
            rhs_copy(piece).start()
        for at in range(ROWS // TILE):
            for piece in range(8):
                for side, sources in enumerate((own, other)):
                    for k in range(8):
                        @pl.when(which[2 * piece + side] == k)
                        def _():
                            lhs_copy(2 * piece + side, sources[k], at).start()
        for piece in range(8):
            rhs_copy(piece).wait()

    for part in range(16):
        lhs_copy(part, own[0], tile).wait()
    out[...] = jnp.dot(
        lhs[pl.ds(pl.multiple_of(tile * TILE, TILE), TILE), :], rhs[...],
        preferred_element_type=jnp.float32,
    )[:, :750]


def multiply(which, own, other, columns):
    return pl.pallas_call(
        multiply_kernel,
        grid=(ROWS // TILE,),
        out_shape=jax.ShapeDtypeStruct((1500, 750), jnp.float32),
        in_specs=[pl.BlockSpec(memory_space=pltpu.SMEM)] + [pl.BlockSpec(memory_space=pl.ANY)] * 24,
        out_specs=pl.BlockSpec((TILE, 750), lambda i: (i, 0)),
        scratch_shapes=[
            pltpu.VMEM((ROWS, 16 * PART), jnp.bfloat16),
            pltpu.VMEM((16 * PART, COLS), jnp.bfloat16),
            pltpu.SemaphoreType.DMA((16, ROWS // TILE)),
            pltpu.SemaphoreType.DMA((8,)),
        ],
        compiler_params=pltpu.CompilerParams(vmem_limit_bytes=48 << 20),
        cost_estimate=pl.CostEstimate(
            flops=2 * 1500 * 750 * 6144, bytes_accessed=33 << 20, transcendentals=0
        ),
    )(which, *own, *other, *columns)


def ring(block, pairs, steps=3):
    out = [block]
    for _ in range(steps):
        out.append(send(out[-1], pairs))
    return out


def body(half_slabs):
    xl, y, xh, z, d = (lax.axis_index(a) for a in AXES)
    rows = jnp.transpose(half_slabs, (1, 0, 2)).reshape(1500, PART)
    rows = jnp.pad(rows, ((0, ROWS - 1500), (0, 0)))
    turned = jnp.transpose(half_slabs, (0, 2, 1)).reshape(PART, 1500)
    low = jnp.pad(turned[:, :750], ((0, 0), (0, COLS - 750)))
    high = jnp.pad(turned[:, 750:], ((0, 0), (0, COLS - 750)))
    keep = jnp.where(d == 0, low, high)
    give = jnp.where(d == 0, high, low)

    near = jnp.concatenate([send(keep, turn(False)), send(give, turn(True))], axis=0)
    far = send(near, X_NEAR)
    columns = ring(near, Y_RING) + ring(far, Y_RING)
    own = ring(rows, Z_RING) + ring(send(rows, X_FAR), Z_RING)
    other = [send(block, CORES) for block in own]

    gamma = jnp.where(d == 0, GAMMA[0], GAMMA[1])
    way = 1 - 2 * d
    which = []
    for half in range(2):
        high_orbital = xl ^ d ^ half
        for step in range(4):
            orbital = gamma - y - z + way * step
            for side in range(2):
                way_of_rows = way if side == 0 else -way
                which.append(4 * (high_orbital ^ xh) + (way_of_rows * (z - orbital)) % 4)
    which = jnp.stack(which).astype(jnp.int32)
    return multiply(which, own, other, columns)


def solution(mesh):
    fine = Mesh(mesh.devices.reshape(SIZES), AXES)
    return jax.shard_map(
        body,
        mesh=fine,
        in_specs=P("d", ("xl", "y"), ("xh", "z")),
        out_specs=P(("xl", "y"), ("xh", "z", "d")),
        check_vma=False,
    )
```

```python
import itertools

import jax
import jax.numpy as jnp
import numpy as np
from jax import lax
from jax.experimental import pallas as pl
from jax.experimental.pallas import tpu as pltpu
from jax.sharding import Mesh
from jax.sharding import PartitionSpec as P

AXES = ("xl", "y", "xh", "z", "d")
SIZES = (2, 4, 2, 4, 2)
GAMMA = (0, 2)
ROWS, COLS, PART = 1536, 768, 384
TILE = 256
COLUMN_STAGE = (0, 0, 1, 0, 0, 1, 2, 1)
ROW_STAGE = ((0, 0, 1, 0, 0, 0, 1, 0), (0, 0, 2, 0, 0, 0, 2, 0))


def perm(target):
    out = []
    for at in itertools.product(*map(range, SIZES)):
        to = target(*at)
        out.append((int(np.ravel_multi_index(at, SIZES)), int(np.ravel_multi_index(to, SIZES))))
    return out


def turn(cross, swap=0):
    def target(xl, y, xh, z, d):
        e = 1 - d if cross else d
        return xh ^ e ^ swap, (GAMMA[e] - y - z) % 4, xl, y, e

    return perm(target)


Z_RING = perm(lambda xl, y, xh, z, d: (xl, y, xh, (z + 1 - 2 * d) % 4, d))
Y_RING = perm(lambda xl, y, xh, z, d: (xl, (y + 1 - 2 * d) % 4, xh, z, d))
Z_BACK = perm(lambda xl, y, xh, z, d: (xl, y, xh, (z - 1 + 2 * d) % 4, d))
Y_BACK = perm(lambda xl, y, xh, z, d: (xl, (y - 1 + 2 * d) % 4, xh, z, d))
X_FAR = perm(lambda xl, y, xh, z, d: (xl, y, 1 - xh, z, d))
X_NEAR = perm(lambda xl, y, xh, z, d: (1 - xl, y, xh, z, d))
CORES = perm(lambda xl, y, xh, z, d: (xl, y, xh, z, 1 - d))


def send(block, pairs):
    return lax.ppermute(block, AXES, pairs)


def multiply_kernel(slots, places, column_places, n_columns, has_total, select, *refs):
    n_rows = 1 + max(place[0] for place in places.values())
    arrays, refs = refs[:n_rows], refs[n_rows:]
    columns, refs = refs[:n_columns], refs[n_columns:]
    total, refs = (refs[0], refs[1:]) if has_total else (None, refs)
    out, lhs, rhs, lhs_sem, rhs_sem = refs
    tile = pl.program_id(0)
    spans = ((0, TILE), (TILE, ROWS - TILE))

    def lhs_copy(slot, place, span):
        start, size = spans[span]
        array, offset = place
        return pltpu.make_async_copy(
            arrays[array].at[pl.ds(offset + start, size)],
            lhs.at[pl.ds(start, size), pl.ds(slot * PART, PART)],
            lhs_sem.at[slot, span],
        )

    def rhs_copy(slot, column):
        return pltpu.make_async_copy(
            columns[column_places[column][0]].at[pl.ds(column_places[column][1] + slots[slot][0] * PART, PART)],
            rhs.at[pl.ds(slot * PART, PART)],
            rhs_sem.at[slot],
        )

    @pl.when(tile == 0)
    def _():
        for span in range(2):
            for slot, (side, row_options, column_options) in enumerate(slots):
                for row in row_options:
                    @pl.when(select[2 * slot] == row)
                    def _():
                        lhs_copy(slot, places[side, row], span).start()
                if span == 0:
                    for column in column_options:
                        @pl.when(select[2 * slot + 1] == column)
                        def _():
                            rhs_copy(slot, column).start()
        for slot, (side, row_options, column_options) in enumerate(slots):
            @pl.when(select[2 * slot] < 0)
            def _():
                lhs[:, slot * PART:(slot + 1) * PART] = jnp.zeros((ROWS, PART), jnp.bfloat16)

    for span in range(2):
        @pl.when(tile == span)
        def _():
            for slot, (side, row_options, column_options) in enumerate(slots):
                if span == 0:
                    rhs_copy(slot, column_options[0]).wait()

                @pl.when(select[2 * slot] >= 0)
                def _():
                    lhs_copy(slot, places[side, row_options[0]], span).wait()

    product = jnp.dot(
        lhs[pl.ds(pl.multiple_of(tile * TILE, TILE), TILE), :], rhs[...],
        preferred_element_type=jnp.float32,
    )[:, :750]
    out[...] = product + total[...] if has_total else product


def multiply(slots, select, places, arrays, column_places, columns, total=None):
    depth = len(slots) * PART
    has_total = total is not None
    block = pl.BlockSpec((TILE, 750), lambda i: (i, 0))
    anywhere = pl.BlockSpec(memory_space=pl.ANY)

    def kernel(*refs):
        multiply_kernel(slots, places, column_places, len(columns), has_total, *refs)

    return pl.pallas_call(
        kernel,
        grid=(ROWS // TILE,),
        out_shape=jax.ShapeDtypeStruct((1500, 750), jnp.float32),
        in_specs=[pl.BlockSpec(memory_space=pltpu.SMEM)]
        + [anywhere] * (len(arrays) + len(columns)) + [block] * has_total,
        out_specs=block,
        scratch_shapes=[
            pltpu.VMEM((ROWS, depth), jnp.bfloat16),
            pltpu.VMEM((depth, COLS), jnp.bfloat16),
            pltpu.SemaphoreType.DMA((len(slots), 2)),
            pltpu.SemaphoreType.DMA((len(slots),)),
        ],
        compiler_params=pltpu.CompilerParams(vmem_limit_bytes=60 << 20),
        cost_estimate=pl.CostEstimate(
            flops=2 * 1500 * 750 * depth,
            bytes_accessed=2 * depth * (ROWS + COLS) + (1 + has_total) * 4 * 1500 * 750,
            transcendentals=0,
        ),
    )(select, *arrays, *columns, *([total] if has_total else []))


def body(half_slabs):
    xl, y, xh, z, d = (lax.axis_index(a) for a in AXES)
    turned = jnp.transpose(half_slabs, (0, 2, 1)).reshape(PART, 1500)
    low = jnp.pad(turned[:, :750], ((0, 0), (0, COLS - 750)))
    high = jnp.pad(turned[:, 750:], ((0, 0), (0, COLS - 750)))
    keep = jnp.where(d == 0, low, high)
    give = jnp.where(d == 0, high, low)
    rows = jnp.transpose(half_slabs, (1, 0, 2)).reshape(1500, PART)
    rows = jnp.pad(rows, ((0, ROWS - 1500), (0, 0)))

    gamma = jnp.where(d == 0, GAMMA[0], GAMMA[1])
    way = 1 - 2 * d

    def row_of(side, column):
        half, step = divmod(column, 4)
        orbital = gamma - z - (y - step * way if half == 0 else y - step * way)
        way_of_rows = way if side == 0 else -way
        return 4 * (xl ^ d ^ half ^ xh) + (way_of_rows * (z - orbital)) % 4

    places = {
        (0, 0): (0, 0), (0, 1): (1, 0), (0, 2): (6, 0), (0, 3): (2, 0),
        (0, 4): (3, 0), (0, 5): (4, 0), (0, 6): (6, ROWS), (0, 7): (5, 0),
        (1, 0): (7, 0), (1, 1): (8, 0), (1, 2): (11, 0), (1, 3): (8, ROWS),
        (1, 4): (9, 0), (1, 5): (9, ROWS), (1, 6): (11, ROWS), (1, 7): (10, 0),
    }
    column_places = [(0, 0), (1, 0), (4, 2 * PART), (2, 0), (3, 0), (4, 0), (6, 0), (5, 0)]

    def add_up(stage, arrays, columns, total=None):
        slots, select = [], []
        for side in range(2):
            for column in range(8):
                if COLUMN_STAGE[column] != stage:
                    continue
                row = row_of(side, column)
                for r in range(8):
                    if ROW_STAGE[side][r] > stage:
                        row = jnp.where(row == r, -1, row)
                slots.append((side, tuple(r for r in range(8) if ROW_STAGE[side][r] <= stage), (column,)))
                select += [row, column]
            for row in range(8):
                options = tuple(c for c in range(8) if COLUMN_STAGE[c] < stage)
                if ROW_STAGE[side][row] != stage or not options:
                    continue
                column, here = options[0], -1
                for c in options:
                    meets = row_of(side, c) == row
                    column, here = jnp.where(meets, c, column), jnp.where(meets, row, here)
                slots.append((side, (row,), options))
                select += [here, column]
        place = {
            key: at for key, at in places.items() if ROW_STAGE[key[0]][key[1]] <= stage
        }
        column_place = {
            c: at for c, at in enumerate(column_places) if COLUMN_STAGE[c] <= stage
        }
        kept = sorted({at[0] for at in place.values()})
        kept_columns = sorted({at[0] for at in column_place.values()})
        return multiply(
            slots,
            jnp.stack([jnp.asarray(v, jnp.int32) for v in select]),
            {key: (kept.index(at[0]), at[1]) for key, at in place.items()},
            [arrays[k] for k in kept],
            {c: (kept_columns.index(at[0]), at[1]) for c, at in column_place.items()},
            [columns[k] for k in kept_columns],
            total,
        )

    def after(block, done):
        return lax.optimization_barrier((block, done))[0]

    rows, keep, give = lax.optimization_barrier((rows, keep, give))
    near, near_other, a1, b0, e0 = send(keep, turn(False)), send(give, turn(True)), send(rows, Z_RING), send(rows, X_FAR), send(rows, CORES)
    a3 = send(after(rows, e0), Z_BACK)
    near, near_other, a1, a3, b0, e0 = lax.optimization_barrier((near, near_other, a1, a3, b0, e0))
    c0 = jnp.concatenate([near, near_other], axis=0)
    d0, c1, c3, b1, e1 = send(c0, X_NEAR), send(c0, Y_RING), send(c0, Y_BACK), send(b0, Z_RING), send(jnp.concatenate([a1, a3]), CORES)
    b3 = send(after(b0, e1), Z_BACK)
    d0, c1, c3, b1, b3, e1 = lax.optimization_barrier((d0, c1, c3, b1, b3, e1))
    up, across, along = send(jnp.concatenate([d0, c1]), Y_RING), send(c3, X_NEAR), send(jnp.concatenate([a1, b1]), Z_RING)
    e2, e3 = send(jnp.concatenate([b0, b1]), CORES), send(b3, CORES)
    total = add_up(0, [rows, a1, a3, b0, b1, b3, None, e0, e1, e2, e3, None], [c0, c1, c3, d0, None, None, None])
    total, up, across, along = lax.optimization_barrier((total, up, across, along))
    d2, e4 = send(up[:2 * PART], Y_RING), send(along, CORES)
    total = add_up(1, [rows, a1, a3, b0, b1, b3, along, e0, e1, e2, e3, None], [c0, c1, c3, d0, up, across, None], total)
    return add_up(2, [rows, a1, a3, b0, b1, b3, along, e0, e1, e2, e3, e4], [c0, c1, c3, d0, up, across, d2], total)


def solution(mesh):
    fine = Mesh(mesh.devices.reshape(SIZES), AXES)
    return jax.shard_map(
        body,
        mesh=fine,
        in_specs=P("d", ("xl", "y"), ("xh", "z")),
        out_specs=P(("xl", "y"), ("xh", "z", "d")),
        check_vma=False,
    )
```

```python
import itertools

import jax
import jax.numpy as jnp
import numpy as np
from jax import lax
from jax.experimental import pallas as pl
from jax.experimental.pallas import tpu as pltpu
from jax.sharding import Mesh
from jax.sharding import PartitionSpec as P

AXES = ("xl", "y", "xh", "z", "d")
SIZES = (2, 4, 2, 4, 2)
BASIS, HALF = 1500, 750
ROWS, COLS, PART = 1536, 768, 384
TILE = 512

ROW_STAGE = ((0, 0, 0, 0, 0, 0, 1, 0), (0, 0, 0, 0, 0, 0, 1, 0))
COLUMN_STAGE = (0, 0, 0, 0, 0, 1, 1, 1)
PLACES = {(0, row): (row, 0) for row in range(8)}
PLACES.update({
    (1, 0): (8, 0), (1, 1): (9, 0), (1, 3): (9, ROWS), (1, 4): (10, 0),
    (1, 5): (10, ROWS), (1, 7): (11, 0), (1, 2): (11, ROWS), (1, 6): (12, 0),
})


def perm(target):
    out = []
    for at in itertools.product(*map(range, SIZES)):
        to = target(*at)
        out.append((int(np.ravel_multi_index(at, SIZES)), int(np.ravel_multi_index(to, SIZES))))
    return out


def turn(cross):
    def target(xl, y, xh, z, d):
        e = 1 - d if cross else d
        return xh ^ e, (2 * e - y - z) % 4, xl, y, e

    return perm(target)


Z_RING = perm(lambda xl, y, xh, z, d: (xl, y, xh, (z + 1 - 2 * d) % 4, d))
Y_RING = perm(lambda xl, y, xh, z, d: (xl, (y + 1 - 2 * d) % 4, xh, z, d))
Z_BACK = perm(lambda xl, y, xh, z, d: (xl, y, xh, (z - 1 + 2 * d) % 4, d))
Y_BACK = perm(lambda xl, y, xh, z, d: (xl, (y - 1 + 2 * d) % 4, xh, z, d))
X_FAR = perm(lambda xl, y, xh, z, d: (xl, y, 1 - xh, z, d))
X_NEAR = perm(lambda xl, y, xh, z, d: (1 - xl, y, xh, z, d))
CORES = perm(lambda xl, y, xh, z, d: (xl, y, xh, z, 1 - d))


def send(block, pairs):
    return lax.ppermute(block, AXES, pairs)


def after(block, done):
    return lax.optimization_barrier((block, done))[0]


def prepare_kernel(spot, slab, rows, keep, give):
    block = slab[...]
    rows[...] = jnp.pad(block, ((0, 0), (0, ROWS - BASIS))).T
    low = jnp.pad(block[:, :HALF], ((0, 0), (0, COLS - HALF)))
    high = jnp.pad(block[:, HALF:], ((0, 0), (0, COLS - HALF)))

    @pl.when(spot[4] == 0)
    def _():
        keep[...] = low
        give[...] = high

    @pl.when(spot[4] == 1)
    def _():
        keep[...] = high
        give[...] = low


def prepare(spot, slab):
    whole = pl.BlockSpec(memory_space=pltpu.VMEM)
    half = jax.ShapeDtypeStruct((PART, COLS), jnp.bfloat16)
    return pl.pallas_call(
        prepare_kernel,
        out_shape=[jax.ShapeDtypeStruct((ROWS, PART), jnp.bfloat16), half, half],
        in_specs=[pl.BlockSpec(memory_space=pltpu.SMEM), whole],
        out_specs=[whole] * 3,
        compiler_params=pltpu.CompilerParams(vmem_limit_bytes=32 << 20),
    )(spot, slab)


def meeting_row(spot, side, column):
    xl, y, xh, z, d = (spot[k] for k in range(5))
    half, step = divmod(column, 4)
    way = 1 - 2 * d
    orbital = 2 * d - y - z + way * step
    steps = (way if side == 0 else -way) * (z - orbital)
    return 4 * (xl ^ d ^ half ^ xh) + (steps & 3)


def slots_of(stage):
    slots = []
    for side in range(2):
        here = tuple(r for r in range(8) if ROW_STAGE[side][r] <= stage)
        slots += [(side, here, (c,)) for c in range(8) if COLUMN_STAGE[c] == stage]
        earlier = tuple(c for c in range(8) if COLUMN_STAGE[c] < stage)
        if earlier:
            slots += [(side, (r,), earlier) for r in here if ROW_STAGE[side][r] == stage]
    return slots


def multiply_kernel(slots, places, column_places, n_columns, has_total, spot, *refs):
    n_rows = 1 + max(place[0] for place in places.values())
    arrays, refs = refs[:n_rows], refs[n_rows:]
    columns, refs = refs[:n_columns], refs[n_columns:]
    total, refs = (refs[0], refs[1:]) if has_total else (None, refs)
    out, lhs, rhs, lhs_sem, rhs_sem = refs
    tile = pl.program_id(0)
    spans = ((0, TILE), (TILE, ROWS - TILE))

    taken = []
    for side, row_options, column_options in slots:
        if len(column_options) == 1:
            met = meeting_row(spot, side, column_options[0])
            row = jnp.int32(-1)
            for r in row_options:
                row = jnp.where(met == r, r, row)
            taken.append((row, jnp.int32(column_options[0])))
        else:
            row, column = jnp.int32(-1), jnp.int32(column_options[0])
            for c in column_options:
                meets = meeting_row(spot, side, c) == row_options[0]
                row = jnp.where(meets, row_options[0], row)
                column = jnp.where(meets, c, column)
            taken.append((row, column))

    def lhs_copy(slot, place, span):
        start, size = spans[span]
        array, offset = place
        return pltpu.make_async_copy(
            arrays[array].at[pl.ds(offset + start, size)],
            lhs.at[pl.ds(start, size), pl.ds(slot * PART, PART)],
            lhs_sem.at[slot, span],
        )

    def rhs_copy(slot, column):
        return pltpu.make_async_copy(
            columns[column_places[column]].at[pl.ds(slots[slot][0] * PART, PART)],
            rhs.at[pl.ds(slot * PART, PART)],
            rhs_sem.at[slot],
        )

    @pl.when(tile == 0)
    def _():
        for span in range(2):
            for slot, (side, row_options, column_options) in enumerate(slots):
                for row in row_options:
                    @pl.when(taken[slot][0] == row)
                    def _():
                        lhs_copy(slot, places[side, row], span).start()
                if span == 0:
                    for column in column_options:
                        @pl.when(taken[slot][1] == column)
                        def _():
                            rhs_copy(slot, column).start()
        for slot in range(len(slots)):
            @pl.when(taken[slot][0] < 0)
            def _():
                lhs[:, slot * PART:(slot + 1) * PART] = jnp.zeros((ROWS, PART), jnp.bfloat16)

    for span in range(2):
        @pl.when(tile == span)
        def _():
            for slot, (side, row_options, column_options) in enumerate(slots):
                if span == 0:
                    rhs_copy(slot, column_options[0]).wait()

                @pl.when(taken[slot][0] >= 0)
                def _():
                    lhs_copy(slot, places[side, row_options[0]], span).wait()

    product = jnp.dot(
        lhs[pl.ds(pl.multiple_of(tile * TILE, TILE), TILE), :], rhs[...],
        preferred_element_type=jnp.float32,
    )[:, :HALF]
    out[...] = product + total[...] if has_total else product


def multiply(stage, spot, arrays, columns, total=None):
    slots = slots_of(stage)
    depth = len(slots) * PART
    has_total = total is not None
    places = {key: at for key, at in PLACES.items() if ROW_STAGE[key[0]][key[1]] <= stage}
    kept = sorted({at[0] for at in places.values()})
    places = {key: (kept.index(at[0]), at[1]) for key, at in places.items()}
    arrays = [arrays[k] for k in kept]
    kept = [c for c in range(8) if COLUMN_STAGE[c] <= stage]
    column_places = {c: k for k, c in enumerate(kept)}
    columns = [columns[c] for c in kept]
    block = pl.BlockSpec((TILE, HALF), lambda i: (i, 0))
    anywhere = pl.BlockSpec(memory_space=pl.ANY)

    def kernel(*refs):
        multiply_kernel(slots, places, column_places, len(columns), has_total, *refs)

    return pl.pallas_call(
        kernel,
        grid=(ROWS // TILE,),
        out_shape=jax.ShapeDtypeStruct((BASIS, HALF), jnp.float32),
        in_specs=[pl.BlockSpec(memory_space=pltpu.SMEM)]
        + [anywhere] * (len(arrays) + len(columns)) + [block] * has_total,
        out_specs=block,
        scratch_shapes=[
            pltpu.VMEM((ROWS, depth), jnp.bfloat16),
            pltpu.VMEM((depth, COLS), jnp.bfloat16),
            pltpu.SemaphoreType.DMA((len(slots), 2)),
            pltpu.SemaphoreType.DMA((len(slots),)),
        ],
        compiler_params=pltpu.CompilerParams(vmem_limit_bytes=60 << 20),
        cost_estimate=pl.CostEstimate(
            flops=2 * BASIS * HALF * depth,
            bytes_accessed=2 * depth * (ROWS + COLS) + (1 + has_total) * 4 * BASIS * HALF,
            transcendentals=0,
        ),
    )(spot, *arrays, *columns, *([total] if has_total else []))


def body(half_slabs):
    spot = jnp.stack([lax.axis_index(a).astype(jnp.int32) for a in AXES])
    slab = jnp.transpose(half_slabs, (0, 2, 1)).reshape(PART, BASIS)
    a0, keep, give = prepare(spot, slab)

    c0, c0_cross, a1, b0, e0 = (
        send(keep, turn(False)), send(give, turn(True)), send(a0, Z_RING), send(a0, X_FAR), send(a0, CORES)
    )
    a3 = send(after(a0, e0), Z_BACK)
    c0, c0_cross, a1, a3, b0, e0 = lax.optimization_barrier((c0, c0_cross, a1, a3, b0, e0))
    c0 = jnp.concatenate([c0, c0_cross], axis=0)

    d0, c1, b1, e1 = (
        send(c0, X_NEAR), send(c0, Y_RING), send(b0, Z_RING), send(jnp.concatenate([a1, a3]), CORES)
    )
    c3, b3 = send(after(c0, e1), Y_BACK), send(after(b0, e1), Z_BACK)
    c2, a2 = send(c1, Y_RING), send(after(a1, b1), Z_RING)
    e2 = send(jnp.concatenate([b0, after(b1, d0)]), CORES)
    d0, c1, c2, c3, b1, b3, a2 = lax.optimization_barrier((d0, c1, c2, c3, b1, b3, a2))

    d1, d3, d2, b2 = send(d0, Y_RING), send(d0, Y_BACK), send(c2, X_NEAR), send(b1, Z_RING)
    e3 = send(jnp.concatenate([b3, a2]), CORES)
    total = multiply(0, spot, [a0, a1, a2, a3, b0, b1, None, b3, e0, e1, e2, e3, None], [c0, c1, c2, c3, d0, None, None, None])
    total, b2 = lax.optimization_barrier((total, b2))
    e4 = send(b2, CORES)
    arrays = [a0, a1, a2, a3, b0, b1, b2, b3, e0, e1, e2, e3, e4]
    return multiply(1, spot, arrays, [c0, c1, c2, c3, d0, d1, d2, d3], total)


def solution(mesh):
    fine = Mesh(mesh.devices.reshape(SIZES), AXES)
    return jax.shard_map(
        body,
        mesh=fine,
        in_specs=P("d", ("xl", "y"), ("xh", "z")),
        out_specs=P(("xl", "y"), ("xh", "z", "d")),
        check_vma=False,
    )
```

```python
import itertools

import jax
import jax.numpy as jnp
import numpy as np
from jax import lax
from jax.experimental import pallas as pl
from jax.experimental.pallas import tpu as pltpu
from jax.sharding import Mesh
from jax.sharding import PartitionSpec as P

AXES = ("xl", "y", "xh", "z", "d")
SIZES = (2, 4, 2, 4, 2)
BASIS, HALF = 1500, 750
ROWS, COLS, PART = 1536, 768, 384
TILE = 512

ROW_STAGE = ((0, 0, 0, 0, 0, 0, 1, 0), (0, 0, 0, 0, 0, 0, 1, 0))
COLUMN_STAGE = (0, 0, 0, 0, 0, 1, 1, 1)
PLACES = {(0, row): (row, 0) for row in range(8)}
PLACES.update({
    (1, 0): (8, 0), (1, 1): (9, 0), (1, 3): (9, ROWS), (1, 4): (10, 0),
    (1, 5): (10, ROWS), (1, 7): (11, 0), (1, 2): (11, ROWS), (1, 6): (12, 0),
})


def perm(target):
    out = []
    for at in itertools.product(*map(range, SIZES)):
        to = target(*at)
        out.append((int(np.ravel_multi_index(at, SIZES)), int(np.ravel_multi_index(to, SIZES))))
    return out


def turn(cross):
    def target(xl, y, xh, z, d):
        e = 1 - d if cross else d
        return xh ^ e, (2 * e - y - z) % 4, xl, y, e

    return perm(target)


Z_RING = perm(lambda xl, y, xh, z, d: (xl, y, xh, (z + 1 - 2 * d) % 4, d))
Y_RING = perm(lambda xl, y, xh, z, d: (xl, (y + 1 - 2 * d) % 4, xh, z, d))
Z_BACK = perm(lambda xl, y, xh, z, d: (xl, y, xh, (z - 1 + 2 * d) % 4, d))
Y_BACK = perm(lambda xl, y, xh, z, d: (xl, (y - 1 + 2 * d) % 4, xh, z, d))
X_FAR = perm(lambda xl, y, xh, z, d: (xl, y, 1 - xh, z, d))
X_NEAR = perm(lambda xl, y, xh, z, d: (1 - xl, y, xh, z, d))
CORES = perm(lambda xl, y, xh, z, d: (xl, y, xh, z, 1 - d))


def send(block, pairs):
    return lax.ppermute(block, AXES, pairs)


def after(block, done):
    return lax.optimization_barrier((block, done))[0]


def prepare_kernel(spot, slab, rows, keep, give):
    block = slab[...]
    rows[...] = jnp.pad(block, ((0, 0), (0, ROWS - BASIS))).T
    low = jnp.pad(block[:, :HALF], ((0, 0), (0, COLS - HALF)))
    high = jnp.pad(block[:, HALF:], ((0, 0), (0, COLS - HALF)))

    @pl.when(spot[4] == 0)
    def _():
        keep[...] = low
        give[...] = high

    @pl.when(spot[4] == 1)
    def _():
        keep[...] = high
        give[...] = low


def prepare(spot, slab):
    whole = pl.BlockSpec(memory_space=pltpu.VMEM)
    half = jax.ShapeDtypeStruct((PART, COLS), jnp.bfloat16)
    return pl.pallas_call(
        prepare_kernel,
        out_shape=[jax.ShapeDtypeStruct((ROWS, PART), jnp.bfloat16), half, half],
        in_specs=[pl.BlockSpec(memory_space=pltpu.SMEM), whole],
        out_specs=[whole] * 3,
        compiler_params=pltpu.CompilerParams(vmem_limit_bytes=12 << 20),
    )(spot, slab)


def meeting_row(spot, side, column):
    xl, y, xh, z, d = (spot[k] for k in range(5))
    half, step = divmod(column, 4)
    way = 1 - 2 * d
    orbital = 2 * d - y - z + way * step
    steps = (way if side == 0 else -way) * (z - orbital)
    return 4 * (xl ^ d ^ half ^ xh) + (steps & 3)


def slots_of(stage):
    slots = []
    for side in range(2):
        here = tuple(r for r in range(8) if ROW_STAGE[side][r] <= stage)
        slots += [(side, here, (c,)) for c in range(8) if COLUMN_STAGE[c] == stage]
        earlier = tuple(c for c in range(8) if COLUMN_STAGE[c] < stage)
        if earlier:
            slots += [(side, (r,), earlier) for r in here if ROW_STAGE[side][r] == stage]
    return slots


def multiply_kernel(slots, places, column_places, n_columns, has_total, spot, *refs):
    n_rows = 1 + max(place[0] for place in places.values())
    arrays, refs = refs[:n_rows], refs[n_rows:]
    columns, refs = refs[:n_columns], refs[n_columns:]
    total, refs = (refs[0], refs[1:]) if has_total else (None, refs)
    out, lhs, rhs, lhs_sem, rhs_sem = refs
    tile = pl.program_id(0)
    spans = ((0, TILE), (TILE, ROWS - TILE))

    taken = []
    for side, row_options, column_options in slots:
        if len(column_options) == 1:
            met = meeting_row(spot, side, column_options[0])
            row = jnp.int32(-1)
            for r in row_options:
                row = jnp.where(met == r, r, row)
            taken.append((row, jnp.int32(column_options[0])))
        else:
            row, column = jnp.int32(-1), jnp.int32(column_options[0])
            for c in column_options:
                meets = meeting_row(spot, side, c) == row_options[0]
                row = jnp.where(meets, row_options[0], row)
                column = jnp.where(meets, c, column)
            taken.append((row, column))

    def lhs_copy(slot, place, span):
        start, size = spans[span]
        array, offset = place
        return pltpu.make_async_copy(
            arrays[array].at[pl.ds(offset + start, size)],
            lhs.at[pl.ds(start, size), pl.ds(slot * PART, PART)],
            lhs_sem.at[slot, span],
        )

    def rhs_copy(slot, column):
        return pltpu.make_async_copy(
            columns[column_places[column]].at[pl.ds(slots[slot][0] * PART, PART)],
            rhs.at[pl.ds(slot * PART, PART)],
            rhs_sem.at[slot],
        )

    @pl.when(tile == 0)
    def _():
        for span in range(2):
            for slot, (side, row_options, column_options) in enumerate(slots):
                for row in row_options:
                    @pl.when(taken[slot][0] == row)
                    def _():
                        lhs_copy(slot, places[side, row], span).start()
                if span == 0:
                    for column in column_options:
                        @pl.when(taken[slot][1] == column)
                        def _():
                            rhs_copy(slot, column).start()
        for slot in range(len(slots)):
            @pl.when(taken[slot][0] < 0)
            def _():
                lhs[:, slot * PART:(slot + 1) * PART] = jnp.zeros((ROWS, PART), jnp.bfloat16)

    for span in range(2):
        @pl.when(tile == span)
        def _():
            for slot, (side, row_options, column_options) in enumerate(slots):
                if span == 0:
                    rhs_copy(slot, column_options[0]).wait()

                @pl.when(taken[slot][0] >= 0)
                def _():
                    lhs_copy(slot, places[side, row_options[0]], span).wait()

    product = jnp.dot(
        lhs[pl.ds(pl.multiple_of(tile * TILE, TILE), TILE), :], rhs[...],
        preferred_element_type=jnp.float32,
    )[:, :HALF]
    out[...] = product + total[...] if has_total else product


def multiply(stage, spot, arrays, columns, total=None):
    slots = slots_of(stage)
    depth = len(slots) * PART
    has_total = total is not None
    places = {key: at for key, at in PLACES.items() if ROW_STAGE[key[0]][key[1]] <= stage}
    kept = sorted({at[0] for at in places.values()})
    places = {key: (kept.index(at[0]), at[1]) for key, at in places.items()}
    arrays = [arrays[k] for k in kept]
    kept = [c for c in range(8) if COLUMN_STAGE[c] <= stage]
    column_places = {c: k for k, c in enumerate(kept)}
    columns = [columns[c] for c in kept]
    block = pl.BlockSpec((TILE, HALF), lambda i: (i, 0))
    anywhere = pl.BlockSpec(memory_space=pl.ANY)

    def kernel(*refs):
        multiply_kernel(slots, places, column_places, len(columns), has_total, *refs)

    return pl.pallas_call(
        kernel,
        grid=(ROWS // TILE,),
        out_shape=jax.ShapeDtypeStruct((BASIS, HALF), jnp.float32),
        in_specs=[pl.BlockSpec(memory_space=pltpu.SMEM)]
        + [anywhere] * (len(arrays) + len(columns)) + [block] * has_total,
        out_specs=block,
        scratch_shapes=[
            pltpu.VMEM((ROWS, depth), jnp.bfloat16),
            pltpu.VMEM((depth, COLS), jnp.bfloat16),
            pltpu.SemaphoreType.DMA((len(slots), 2)),
            pltpu.SemaphoreType.DMA((len(slots),)),
        ],
        compiler_params=pltpu.CompilerParams(vmem_limit_bytes=23 << 20),
        cost_estimate=pl.CostEstimate(
            flops=2 * BASIS * HALF * depth,
            bytes_accessed=2 * depth * (ROWS + COLS) + (1 + has_total) * 4 * BASIS * HALF,
            transcendentals=0,
        ),
    )(spot, *arrays, *columns, *([total] if has_total else []))


def body(half_slabs):
    spot = jnp.stack([lax.axis_index(a).astype(jnp.int32) for a in AXES])
    slab = jnp.transpose(half_slabs, (0, 2, 1)).reshape(PART, BASIS)
    a0, keep, give = prepare(spot, slab)

    c0, c0_cross, a1, b0, e0 = (
        send(keep, turn(False)), send(give, turn(True)), send(a0, Z_RING), send(a0, X_FAR), send(a0, CORES)
    )
    a3 = send(after(a0, e0), Z_BACK)
    c0, c0_cross, a1, a3, b0, e0 = lax.optimization_barrier((c0, c0_cross, a1, a3, b0, e0))
    c0 = jnp.concatenate([c0, c0_cross], axis=0)

    d0, c1, b1, e1 = (
        send(c0, X_NEAR), send(c0, Y_RING), send(b0, Z_RING), send(jnp.concatenate([a1, a3]), CORES)
    )
    c3, b3 = send(c0, Y_BACK), send(b0, Z_BACK)
    c2, a2 = send(c1, Y_RING), send(after(a1, b1), Z_RING)
    e2 = send(jnp.concatenate([b0, after(b1, d0)]), CORES)
    d0, c1, c2, c3, b1, b3, a2 = lax.optimization_barrier((d0, c1, c2, c3, b1, b3, a2))


    d1, d3, d2, b2 = send(d0, Y_RING), send(d0, Y_BACK), send(c2, X_NEAR), send(b1, Z_RING)
    e3 = send(jnp.concatenate([b3, a2]), CORES)
    total = multiply(0, spot, [a0, a1, a2, a3, b0, b1, None, b3, e0, e1, e2, e3, None], [c0, c1, c2, c3, d0, None, None, None])
    total, b2 = lax.optimization_barrier((total, b2))
    e4 = send(b2, CORES)
    arrays = [a0, a1, a2, a3, b0, b1, b2, b3, e0, e1, e2, e3, e4]
    return multiply(1, spot, arrays, [c0, c1, c2, c3, d0, d1, d2, d3], total)


def solution(mesh):
    fine = Mesh(mesh.devices.reshape(SIZES), AXES)
    return jax.shard_map(
        body,
        mesh=fine,
        in_specs=P("d", ("xl", "y"), ("xh", "z")),
        out_specs=P(("xl", "y"), ("xh", "z", "d")),
        check_vma=False,
    )
```

```python
import itertools

import jax
import jax.numpy as jnp
import numpy as np
from jax import lax
from jax.experimental import pallas as pl
from jax.experimental.pallas import tpu as pltpu
from jax.sharding import Mesh
from jax.sharding import PartitionSpec as P

AXES = ("xl", "y", "xh", "z", "d")
SIZES = (2, 4, 2, 4, 2)
BASIS, HALF = 1500, 750
ROWS, COLS, PART = 1536, 768, 384
TILE = 384

ROW_STAGE = ((0, 0, 0, 0, 0, 0, 1, 0), (0, 0, 0, 0, 0, 0, 1, 0))
COLUMN_STAGE = (0, 0, 0, 0, 0, 1, 1, 1)
PLACES = {(0, row): (row, 0) for row in range(8)}
PLACES.update({
    (1, 0): (8, 0), (1, 1): (9, 0), (1, 2): (9, ROWS), (1, 3): (10, 0),
    (1, 4): (10, ROWS), (1, 5): (11, 0), (1, 7): (11, ROWS), (1, 6): (12, 0),
})


def perm(target):
    out = []
    for at in itertools.product(*map(range, SIZES)):
        to = target(*at)
        out.append((int(np.ravel_multi_index(at, SIZES)), int(np.ravel_multi_index(to, SIZES))))
    return out


def turn(cross):
    def target(xl, y, xh, z, d):
        e = 1 - d if cross else d
        return xh ^ e, (2 * e - y - z) % 4, xl, y, e

    return perm(target)


Z_RING = perm(lambda xl, y, xh, z, d: (xl, y, xh, (z + 1 - 2 * d) % 4, d))
Y_RING = perm(lambda xl, y, xh, z, d: (xl, (y + 1 - 2 * d) % 4, xh, z, d))
Z_BACK = perm(lambda xl, y, xh, z, d: (xl, y, xh, (z - 1 + 2 * d) % 4, d))
Y_BACK = perm(lambda xl, y, xh, z, d: (xl, (y - 1 + 2 * d) % 4, xh, z, d))
X_FAR = perm(lambda xl, y, xh, z, d: (xl, y, 1 - xh, z, d))
X_NEAR = perm(lambda xl, y, xh, z, d: (1 - xl, y, xh, z, d))
CORES = perm(lambda xl, y, xh, z, d: (xl, y, xh, z, 1 - d))


def send(block, pairs):
    return lax.ppermute(block, AXES, pairs)


def after(block, done):
    return lax.optimization_barrier((block, done))[0]


def prepare_kernel(spot, slab, rows, keep, give):
    block = slab[...]
    rows[...] = jnp.pad(block, ((0, 0), (0, ROWS - BASIS))).T
    low = jnp.pad(block[:, :HALF], ((0, 0), (0, COLS - HALF)))
    high = jnp.pad(block[:, HALF:], ((0, 0), (0, COLS - HALF)))

    @pl.when(spot[4] == 0)
    def _():
        keep[...] = low
        give[...] = high

    @pl.when(spot[4] == 1)
    def _():
        keep[...] = high
        give[...] = low


def prepare(spot, slab):
    whole = pl.BlockSpec(memory_space=pltpu.VMEM)
    half = jax.ShapeDtypeStruct((PART, COLS), jnp.bfloat16)
    return pl.pallas_call(
        prepare_kernel,
        out_shape=[jax.ShapeDtypeStruct((ROWS, PART), jnp.bfloat16), half, half],
        in_specs=[pl.BlockSpec(memory_space=pltpu.SMEM), whole],
        out_specs=[whole] * 3,
        compiler_params=pltpu.CompilerParams(vmem_limit_bytes=12 << 20),
    )(spot, slab)


def meeting_row(spot, side, column):
    xl, y, xh, z, d = (spot[k] for k in range(5))
    half, step = divmod(column, 4)
    way = 1 - 2 * d
    orbital = 2 * d - y - z + way * step
    steps = (way if side == 0 else -way) * (z - orbital)
    return 4 * (xl ^ d ^ half ^ xh) + (steps & 3)


def slots_of(stage):
    slots = []
    for side in range(2):
        here = tuple(r for r in range(8) if ROW_STAGE[side][r] <= stage)
        slots += [(side, here, (c,)) for c in range(8) if COLUMN_STAGE[c] == stage]
        earlier = tuple(c for c in range(8) if COLUMN_STAGE[c] < stage)
        if earlier:
            slots += [(side, (r,), earlier) for r in here if ROW_STAGE[side][r] == stage]
    return slots


def multiply_kernel(slots, places, column_places, n_columns, has_total, spot, *refs):
    n_rows = 1 + max(place[0] for place in places.values())
    arrays, refs = refs[:n_rows], refs[n_rows:]
    columns, refs = refs[:n_columns], refs[n_columns:]
    total, refs = (refs[0], refs[1:]) if has_total else (None, refs)
    out, lhs, rhs, lhs_sem, rhs_sem = refs
    tile = pl.program_id(0)
    spans = ((0, TILE), (TILE, ROWS - TILE))

    taken = []
    for side, row_options, column_options in slots:
        if len(column_options) == 1:
            met = meeting_row(spot, side, column_options[0])
            row = jnp.int32(-1)
            for r in row_options:
                row = jnp.where(met == r, r, row)
            taken.append((row, jnp.int32(column_options[0])))
        else:
            row, column = jnp.int32(-1), jnp.int32(column_options[0])
            for c in column_options:
                meets = meeting_row(spot, side, c) == row_options[0]
                row = jnp.where(meets, row_options[0], row)
                column = jnp.where(meets, c, column)
            taken.append((row, column))

    def lhs_copy(slot, place, span):
        start, size = spans[span]
        array, offset = place
        return pltpu.make_async_copy(
            arrays[array].at[pl.ds(offset + start, size)],
            lhs.at[pl.ds(start, size), pl.ds(slot * PART, PART)],
            lhs_sem.at[slot, span],
        )

    def rhs_copy(slot, column):
        return pltpu.make_async_copy(
            columns[column_places[column]].at[pl.ds(slots[slot][0] * PART, PART)],
            rhs.at[pl.ds(slot * PART, PART)],
            rhs_sem.at[slot],
        )

    @pl.when(tile == 0)
    def _():
        for span in range(2):
            for slot, (side, row_options, column_options) in enumerate(slots):
                for row in row_options:
                    @pl.when(taken[slot][0] == row)
                    def _():
                        lhs_copy(slot, places[side, row], span).start()
                if span == 0:
                    for column in column_options:
                        @pl.when(taken[slot][1] == column)
                        def _():
                            rhs_copy(slot, column).start()
        for slot in range(len(slots)):
            @pl.when(taken[slot][0] < 0)
            def _():
                lhs[:, slot * PART:(slot + 1) * PART] = jnp.zeros((ROWS, PART), jnp.bfloat16)

    for span in range(2):
        @pl.when(tile == span)
        def _():
            for slot, (side, row_options, column_options) in enumerate(slots):
                if span == 0:
                    rhs_copy(slot, column_options[0]).wait()

                @pl.when(taken[slot][0] >= 0)
                def _():
                    lhs_copy(slot, places[side, row_options[0]], span).wait()

    product = jnp.dot(
        lhs[pl.ds(pl.multiple_of(tile * TILE, TILE), TILE), :], rhs[...],
        preferred_element_type=jnp.float32,
    )[:, :HALF]
    out[...] = product + total[...] if has_total else product


def multiply(stage, spot, arrays, columns, total=None):
    slots = slots_of(stage)
    depth = len(slots) * PART
    has_total = total is not None
    places = {key: at for key, at in PLACES.items() if ROW_STAGE[key[0]][key[1]] <= stage}
    kept = sorted({at[0] for at in places.values()})
    places = {key: (kept.index(at[0]), at[1]) for key, at in places.items()}
    arrays = [arrays[k] for k in kept]
    kept = [c for c in range(8) if COLUMN_STAGE[c] <= stage]
    column_places = {c: k for k, c in enumerate(kept)}
    columns = [columns[c] for c in kept]
    block = pl.BlockSpec((TILE, HALF), lambda i: (i, 0))
    anywhere = pl.BlockSpec(memory_space=pl.ANY)

    def kernel(*refs):
        multiply_kernel(slots, places, column_places, len(columns), has_total, *refs)

    return pl.pallas_call(
        kernel,
        grid=(ROWS // TILE,),
        out_shape=jax.ShapeDtypeStruct((BASIS, HALF), jnp.float32),
        in_specs=[pl.BlockSpec(memory_space=pltpu.SMEM)]
        + [anywhere] * (len(arrays) + len(columns)) + [block] * has_total,
        out_specs=block,
        scratch_shapes=[
            pltpu.VMEM((ROWS, depth), jnp.bfloat16),
            pltpu.VMEM((depth, COLS), jnp.bfloat16),
            pltpu.SemaphoreType.DMA((len(slots), 2)),
            pltpu.SemaphoreType.DMA((len(slots),)),
        ],
        compiler_params=pltpu.CompilerParams(vmem_limit_bytes=23 << 20),
        cost_estimate=pl.CostEstimate(
            flops=2 * BASIS * HALF * depth,
            bytes_accessed=2 * depth * (ROWS + COLS) + (1 + has_total) * 4 * BASIS * HALF,
            transcendentals=0,
        ),
    )(spot, *arrays, *columns, *([total] if has_total else []))


def body(half_slabs):
    spot = jnp.stack([lax.axis_index(a).astype(jnp.int32) for a in AXES])
    slab = jnp.transpose(half_slabs, (0, 2, 1)).reshape(PART, BASIS)
    a0, keep, give = prepare(spot, slab)

    c0, c0_cross, a1, e0 = (
        send(keep, turn(False)), send(give, turn(True)), send(a0, Z_RING), send(a0, CORES)
    )
    own, c0, c0_cross, e0 = lax.optimization_barrier((a0, c0, c0_cross, e0))
    c0 = jnp.concatenate([c0, c0_cross], axis=0)

    b0, c1, c3, a2, a3 = (
        send(own, X_FAR), send(c0, Y_RING), send(c0, Y_BACK), send(after(a1, c0_cross), Z_RING), send(own, Z_BACK)
    )
    c0, b0, c1, c3, a2, a3 = lax.optimization_barrier((c0, b0, c1, c3, a2, a3))

    d0, b1, c2 = send(c0, X_NEAR), send(b0, Z_RING), send(c1, Y_RING)
    e1, e2 = send(jnp.concatenate([a1, a2]), CORES), send(jnp.concatenate([a3, b0]), CORES)
    b3 = send(after(b0, e1), Z_BACK)
    d0, b1, b3, c2, e1, e2 = lax.optimization_barrier((d0, b1, b3, c2, e1, e2))

    d1, d3, d2, b2 = send(d0, Y_RING), send(d0, Y_BACK), send(c2, X_NEAR), send(b1, Z_RING)
    e3 = send(jnp.concatenate([b1, b3]), CORES)
    total = multiply(0, spot, [a0, a1, a2, a3, b0, b1, None, b3, e0, e1, e2, e3, None], [c0, c1, c2, c3, d0, None, None, None])
    total, b2 = lax.optimization_barrier((total, b2))
    e4 = send(b2, CORES)
    arrays = [a0, a1, a2, a3, b0, b1, b2, b3, e0, e1, e2, e3, e4]
    return multiply(1, spot, arrays, [c0, c1, c2, c3, d0, d1, d2, d3], total)


def solution(mesh):
    fine = Mesh(mesh.devices.reshape(SIZES), AXES)
    return jax.shard_map(
        body,
        mesh=fine,
        in_specs=P("d", ("xl", "y"), ("xh", "z")),
        out_specs=P(("xl", "y"), ("xh", "z", "d")),
        check_vma=False,
    )
```

```python
import itertools

import jax
import jax.numpy as jnp
import numpy as np
from jax import lax
from jax.experimental import pallas as pl
from jax.experimental.pallas import tpu as pltpu
from jax.sharding import Mesh
from jax.sharding import PartitionSpec as P

AXES = ("xl", "y", "xh", "z", "d")
SIZES = (2, 4, 2, 4, 2)
BASIS, HALF = 1500, 750
ROWS, COLS, PART = 1536, 768, 384
TILE = 384

ROW_STAGE = ((0, 0, 0, 0, 0, 0, 1, 0), (0, 0, 0, 0, 0, 0, 1, 0))
COLUMN_STAGE = (0, 0, 0, 0, 0, 1, 1, 1)
PLACES = {(0, row): (row, 0) for row in range(8)}
PLACES.update({
    (1, 0): (8, 0), (1, 1): (9, 0), (1, 2): (9, ROWS), (1, 3): (10, 0),
    (1, 4): (10, ROWS), (1, 5): (11, 0), (1, 7): (11, ROWS), (1, 6): (12, 0),
})


def perm(target):
    out = []
    for at in itertools.product(*map(range, SIZES)):
        to = target(*at)
        out.append((int(np.ravel_multi_index(at, SIZES)), int(np.ravel_multi_index(to, SIZES))))
    return out


def turn(cross):
    def target(xl, y, xh, z, d):
        e = 1 - d if cross else d
        return xh ^ e, (2 * e - y - z) % 4, xl, y, e

    return perm(target)


Z_RING = perm(lambda xl, y, xh, z, d: (xl, y, xh, (z + 1 - 2 * d) % 4, d))
Y_RING = perm(lambda xl, y, xh, z, d: (xl, (y + 1 - 2 * d) % 4, xh, z, d))
Z_BACK = perm(lambda xl, y, xh, z, d: (xl, y, xh, (z - 1 + 2 * d) % 4, d))
Y_BACK = perm(lambda xl, y, xh, z, d: (xl, (y - 1 + 2 * d) % 4, xh, z, d))
X_FAR = perm(lambda xl, y, xh, z, d: (xl, y, 1 - xh, z, d))
X_NEAR = perm(lambda xl, y, xh, z, d: (1 - xl, y, xh, z, d))
CORES = perm(lambda xl, y, xh, z, d: (xl, y, xh, z, 1 - d))


def send(block, pairs):
    return lax.ppermute(block, AXES, pairs)


def after(block, done):
    return lax.optimization_barrier((block, done))[0]


def prepare_kernel(spot, slab, rows, keep, give):
    block = slab[...]
    rows[...] = jnp.pad(block, ((0, 0), (0, ROWS - BASIS))).T
    low = jnp.pad(block[:, :HALF], ((0, 0), (0, COLS - HALF)))
    high = jnp.pad(block[:, HALF:], ((0, 0), (0, COLS - HALF)))

    @pl.when(spot[4] == 0)
    def _():
        keep[...] = low
        give[...] = high

    @pl.when(spot[4] == 1)
    def _():
        keep[...] = high
        give[...] = low


def prepare(spot, slab):
    whole = pl.BlockSpec(memory_space=pltpu.VMEM)
    half = jax.ShapeDtypeStruct((PART, COLS), jnp.bfloat16)
    return pl.pallas_call(
        prepare_kernel,
        out_shape=[jax.ShapeDtypeStruct((ROWS, PART), jnp.bfloat16), half, half],
        in_specs=[pl.BlockSpec(memory_space=pltpu.SMEM), whole],
        out_specs=[whole] * 3,
        compiler_params=pltpu.CompilerParams(vmem_limit_bytes=12 << 20),
    )(spot, slab)


def meeting_row(spot, side, column):
    xl, y, xh, z, d = (spot[k] for k in range(5))
    half, step = divmod(column, 4)
    way = 1 - 2 * d
    orbital = 2 * d - y - z + way * step
    steps = (way if side == 0 else -way) * (z - orbital)
    return 4 * (xl ^ d ^ half ^ xh) + (steps & 3)


def slots_of(stage):
    slots = []
    for side in range(2):
        here = tuple(r for r in range(8) if ROW_STAGE[side][r] <= stage)
        slots += [(side, here, (c,)) for c in range(8) if COLUMN_STAGE[c] == stage]
        earlier = tuple(c for c in range(8) if COLUMN_STAGE[c] < stage)
        if earlier:
            slots += [(side, (r,), earlier) for r in here if ROW_STAGE[side][r] == stage]
    return slots


def multiply_kernel(slots, places, column_places, n_columns, has_total, spot, *refs):
    n_rows = 1 + max(place[0] for place in places.values())
    arrays, refs = refs[:n_rows], refs[n_rows:]
    columns, refs = refs[:n_columns], refs[n_columns:]
    total, refs = (refs[0], refs[1:]) if has_total else (None, refs)
    out, lhs, rhs, lhs_sem, rhs_sem = refs
    tile = pl.program_id(0)
    spans = ((0, TILE), (TILE, ROWS - TILE))

    taken = []
    for side, row_options, column_options in slots:
        if len(column_options) == 1:
            met = meeting_row(spot, side, column_options[0])
            row = jnp.int32(-1)
            for r in row_options:
                row = jnp.where(met == r, r, row)
            taken.append((row, jnp.int32(column_options[0])))
        else:
            row, column = jnp.int32(-1), jnp.int32(column_options[0])
            for c in column_options:
                meets = meeting_row(spot, side, c) == row_options[0]
                row = jnp.where(meets, row_options[0], row)
                column = jnp.where(meets, c, column)
            taken.append((row, column))

    def lhs_copy(slot, place, span):
        start, size = spans[span]
        array, offset = place
        return pltpu.make_async_copy(
            arrays[array].at[pl.ds(offset + start, size)],
            lhs.at[pl.ds(start, size), pl.ds(slot * PART, PART)],
            lhs_sem.at[slot, span],
        )

    def rhs_copy(slot, column):
        return pltpu.make_async_copy(
            columns[column_places[column]].at[pl.ds(slots[slot][0] * PART, PART)],
            rhs.at[pl.ds(slot * PART, PART)],
            rhs_sem.at[slot],
        )

    @pl.when(tile == 0)
    def _():
        for span in range(2):
            for slot, (side, row_options, column_options) in enumerate(slots):
                for row in row_options:
                    @pl.when(taken[slot][0] == row)
                    def _():
                        lhs_copy(slot, places[side, row], span).start()
                if span == 0:
                    for column in column_options:
                        @pl.when(taken[slot][1] == column)
                        def _():
                            rhs_copy(slot, column).start()
        for slot in range(len(slots)):
            @pl.when(taken[slot][0] < 0)
            def _():
                lhs[:, slot * PART:(slot + 1) * PART] = jnp.zeros((ROWS, PART), jnp.bfloat16)

    for span in range(2):
        @pl.when(tile == span)
        def _():
            for slot, (side, row_options, column_options) in enumerate(slots):
                if span == 0:
                    rhs_copy(slot, column_options[0]).wait()

                @pl.when(taken[slot][0] >= 0)
                def _():
                    lhs_copy(slot, places[side, row_options[0]], span).wait()

    product = jnp.dot(
        lhs[pl.ds(pl.multiple_of(tile * TILE, TILE), TILE), :], rhs[...],
        preferred_element_type=jnp.float32,
    )[:, :HALF]
    out[...] = product + total[...] if has_total else product


def multiply(stage, spot, arrays, columns, total=None):
    slots = slots_of(stage)
    depth = len(slots) * PART
    has_total = total is not None
    places = {key: at for key, at in PLACES.items() if ROW_STAGE[key[0]][key[1]] <= stage}
    kept = sorted({at[0] for at in places.values()})
    places = {key: (kept.index(at[0]), at[1]) for key, at in places.items()}
    arrays = [arrays[k] for k in kept]
    kept = [c for c in range(8) if COLUMN_STAGE[c] <= stage]
    column_places = {c: k for k, c in enumerate(kept)}
    columns = [columns[c] for c in kept]
    block = pl.BlockSpec((TILE, HALF), lambda i: (i, 0))
    anywhere = pl.BlockSpec(memory_space=pl.ANY)

    def kernel(*refs):
        multiply_kernel(slots, places, column_places, len(columns), has_total, *refs)

    return pl.pallas_call(
        kernel,
        grid=(ROWS // TILE,),
        out_shape=jax.ShapeDtypeStruct((BASIS, HALF), jnp.float32),
        in_specs=[pl.BlockSpec(memory_space=pltpu.SMEM)]
        + [anywhere] * (len(arrays) + len(columns)) + [block] * has_total,
        out_specs=block,
        scratch_shapes=[
            pltpu.VMEM((ROWS, depth), jnp.bfloat16),
            pltpu.VMEM((depth, COLS), jnp.bfloat16),
            pltpu.SemaphoreType.DMA((len(slots), 2)),
            pltpu.SemaphoreType.DMA((len(slots),)),
        ],
        compiler_params=pltpu.CompilerParams(vmem_limit_bytes=23 << 20),
        cost_estimate=pl.CostEstimate(
            flops=2 * BASIS * HALF * depth,
            bytes_accessed=2 * depth * (ROWS + COLS) + (1 + has_total) * 4 * BASIS * HALF,
            transcendentals=0,
        ),
    )(spot, *arrays, *columns, *([total] if has_total else []))


def body(half_slabs):
    spot = jnp.stack([lax.axis_index(a).astype(jnp.int32) for a in AXES])
    slab = jnp.transpose(half_slabs, (0, 2, 1)).reshape(PART, BASIS)
    a0, keep, give = prepare(spot, slab)

    c0, c0_cross, a1, e0 = (
        send(keep, turn(False)), send(give, turn(True)), send(a0, Z_RING), send(a0, CORES)
    )
    own, c0, c0_cross, e0 = lax.optimization_barrier((a0, c0, c0_cross, e0))
    c0 = jnp.concatenate([c0, c0_cross], axis=0)

    b0, c1, c3, a2, a3 = (
        send(own, X_FAR), send(c0, Y_RING), send(c0, Y_BACK), send(after(a1, c0_cross), Z_RING), send(own, Z_BACK)
    )
    e1 = send(jnp.concatenate([a1, a2]), CORES)
    c0, b0, c1, c3, a2, a3 = lax.optimization_barrier((c0, b0, c1, c3, a2, a3))

    d0, b1, c2 = send(c0, X_NEAR), send(b0, Z_RING), send(c1, Y_RING)
    e2 = send(jnp.concatenate([a3, b0]), CORES)
    b3 = send(after(b0, e1), Z_BACK)
    d0, b1, b3, c2, e1, e2 = lax.optimization_barrier((d0, b1, b3, c2, e1, e2))

    d1, d3, d2, b2 = send(d0, Y_RING), send(d0, Y_BACK), send(c2, X_NEAR), send(b1, Z_RING)
    e3 = send(jnp.concatenate([b1, b3]), CORES)
    total = multiply(0, spot, [a0, a1, a2, a3, b0, b1, None, b3, e0, e1, e2, e3, None], [c0, c1, c2, c3, d0, None, None, None])
    total, b2 = lax.optimization_barrier((total, b2))
    e4 = send(b2, CORES)
    arrays = [a0, a1, a2, a3, b0, b1, b2, b3, e0, e1, e2, e3, e4]
    return multiply(1, spot, arrays, [c0, c1, c2, c3, d0, d1, d2, d3], total)


def solution(mesh):
    fine = Mesh(mesh.devices.reshape(SIZES), AXES)
    return jax.shard_map(
        body,
        mesh=fine,
        in_specs=P("d", ("xl", "y"), ("xh", "z")),
        out_specs=P(("xl", "y"), ("xh", "z", "d")),
        check_vma=False,
    )
```
